32 devices in a mesh: seq: 8 (over z, y), head: 4 (over x, core).
Axes of the slice: x: 2, y: 2, z: 4, core: 2. Of those that a mesh axis runs over, the one named last changes fastest.
Arguments:
- queries: bfloat16 [4096, 4096], P('seq', 'head'), may hold values from -40 to 40
- stretch_keys: bfloat16 [4096, 4096], P('seq', 'head'), may hold values from -6 to 6
- stretch_values: bfloat16 [4096, 4096], P('seq', 'head'), may hold values from -6 to 6
- segment_ids: int32 [4096], replicated, may hold values from 0 to 7, never falling along the last dimension, each value on 1 to 3072 neighbouring positions
- block_live: int32 [8, 8], replicated, may hold values 0 or 1
- out_weight: bfloat16 [4096, 7168], P('head'), may hold values from -0.09375 to 0.09375
- cache_keys: bfloat16 [4, 4096, 4096], P(None, 'seq', 'head'), may hold values from -6 to 6
- cache_values: bfloat16 [4, 4096, 4096], P(None, 'seq', 'head'), may hold values from -6 to 6
- page_table: int32 [256], replicated, may hold values from 0 to 255, as said below
Outputs:
- attn_out: bfloat16 [4096, 4096], P('seq', 'head')
- proj_out: bfloat16 [4096, 7168], P(('seq', 'head'))
- decode_keys: bfloat16 [4, 256, 16, 4096], P(None, 'seq', None, 'head')
- decode_values: bfloat16 [4, 256, 16, 4096], P(None, 'seq', None, 'head')
The draws below stay inside these ranges and needn't reach their ends.
Inputs may be any that keep to these rules, and one draw needn't show every extreme that they name: page_table holds each of 0 to 255 once; the slot s belongs to request group s // 32; each aligned run of 4 pages of one token block goes to one group, and the 8 runs of one token block go to 8 different groups.
All inputs are finite; a program needn't handle non-finite values.
Results may differ from the reference program's by a relative error of at most 0.018.
Values may be sent and summed in bfloat16 or wider, within the bound.
A program may use at most 192 MiB of HBM per device.

```python
import math
import jax
import jax.numpy as jnp
import numpy as np
from jax import lax

D = 7168
HEADS = 32
HD = 128
T_DEV = 512
PAGE = 16
LAYERS_KV = 4
NBLK = 8
TOKENS = 4096
PAGES_DEV = 32
NPAGES = 256
CAP = 4
N_HEAD = 4


def drawn_pair(key):
    base_keys = jax.random.fold_in(key, 71)
    base_queries = jax.random.fold_in(key, 72)
    full_shape = (TOKENS, HEADS * HD)
    key_draw = jnp.clip(jax.random.normal(base_keys, full_shape, jnp.float32), -6.0, 6.0)
    query_draw = jnp.clip(jax.random.normal(base_queries, full_shape, jnp.float32), -6.0, 6.0)
    return (query_draw, key_draw)


def draw_queries(key, part):
    return drawn_pair(key)[0].astype(jnp.bfloat16)


def draw_stretch_keys(key, part):
    return drawn_pair(key)[1].astype(jnp.bfloat16)


def draw_page_table(key, part):
    offsets = jax.random.permutation(jax.random.fold_in(key, 81), NBLK)
    order_keys = jax.random.split(jax.random.fold_in(key, 82), NBLK)
    within = jax.vmap(lambda group_key: jax.random.permutation(group_key, PAGES_DEV))(order_keys)
    page_ids = jnp.arange(NPAGES)
    source = page_ids // PAGES_DEV
    local_idx = page_ids % PAGES_DEV
    run_idx = local_idx // CAP
    groups = (source + offsets[run_idx]) % NBLK
    slot_ids = within[groups, local_idx]
    return (groups * PAGES_DEV + slot_ids).astype(jnp.int32)


def touch_ends(entries, own_key, least, high):
    longest = entries.shape.index(max(entries.shape))
    spots = []
    for shift in (0, 1):
        where = [jax.random.randint(jax.random.fold_in(own_key, axis), (), 0, length) for axis, length in enumerate(entries.shape)]
        where[longest] = (where[longest] + shift) % entries.shape[longest]
        spots.append(tuple(where))
    return entries.at[spots[0]].set(least).at[spots[1]].set(high)


def shard_levels(key, extent, cuts, low, top_value):
    def one(position, blocks):
        draws = jax.random.uniform(jax.random.fold_in(jax.random.fold_in(key, 6), position), (blocks,), jnp.float32, low / len(cuts), top_value / len(cuts))
        return jnp.repeat(jnp.exp(draws), extent[position] // blocks).reshape((-1,) + (1,) * (len(extent) - position - 1))

    factor_of = one(*cuts[0])
    for cut in cuts[1:]:
        factor_of = factor_of * one(*cut)
    return factor_of


def length_profile(count, total, reach, lean):
    portions = [(1 << 20) // math.isqrt(rank ** lean) + 1 for rank in range(2, count + 1)]
    surplus, given = total - reach - (count - 1), [1] * (count - 1)
    while surplus > 0:
        candidates = [i for i in range(count - 1) if given[i] < reach]
        whole, budget = sum([portions[i] for i in candidates]), surplus
        for i in candidates:
            extra = min(reach - given[i], max(1, budget * portions[i] // whole), surplus)
            given[i] = given[i] + extra
            surplus = surplus - extra
    return np.array([reach] + given)


def ragged(rng, count, total, limit, lean):
    if count == 2:
        one = jax.random.randint(rng, (), max(1, total - limit), min(limit, total - 1) + 1)
        return jnp.stack([one, total - one])
    lengths = jnp.asarray(length_profile(count, total, limit, lean), jnp.int32)
    couples = (count - 1) // 2
    source_of, sink = lengths[1:1 + 2 * couples:2], lengths[2:2 + 2 * couples:2]
    slack = jnp.minimum(source_of - 1, limit - sink)
    shifted = jax.random.randint(jax.random.fold_in(rng, 1), (couples,), 0, 1 << 20) % (slack + 1)
    lengths = lengths.at[1:1 + 2 * couples:2].set(source_of - shifted).at[2:2 + 2 * couples:2].set(sink + shifted)
    return lengths[jax.random.permutation(jax.random.fold_in(rng, 2), count)]


def scatter_about(key, shape, width, bound, cuts=(), kind=jnp.bfloat16):
    result = width * jax.random.normal(key, shape, jnp.float32)
    if cuts:
        result = result * shard_levels(key, shape, cuts, -0.22, 0.18)
    return jnp.clip(result, -bound, bound).astype(kind)


def setup_inputs(seed: int = 0) -> dict:
    keys = jax.random.split(jax.random.key(seed), 10)
    return {
        "queries": draw_queries(jax.random.fold_in(keys[9], 71), 0),
        "stretch_keys": draw_stretch_keys(jax.random.fold_in(keys[9], 71), 0),
        "stretch_values": scatter_about(keys[2], (TOKENS, HEADS * HD), 1.0, 6.0, ((0, 8), (1, 4))),
        "segment_ids": jnp.searchsorted(jnp.cumsum(ragged(keys[3], 8, TOKENS, 3 * TOKENS // 4, 1)), jnp.arange(TOKENS), side="right").astype(jnp.int32),
        "block_live": touch_ends((jax.random.randint(keys[4], (NBLK, NBLK), 0, 4) < 3).astype(jnp.int32), jax.random.fold_in(keys[4], 1), 0, 1),
        "out_weight": scatter_about(keys[5], (HEADS * HD, D), (HEADS * HD) ** -0.5, 0.09375, ((0, 4),)),
        "cache_keys": scatter_about(keys[6], (LAYERS_KV, TOKENS, HEADS * HD), 1.0, 6.0, ((1, 8), (2, 4))),
        "cache_values": scatter_about(keys[7], (LAYERS_KV, TOKENS, HEADS * HD), 1.0, 6.0, ((1, 8), (2, 4))),
        "page_table": draw_page_table(jax.random.fold_in(keys[9], 71), 0),
    }


def block_allowed(q_block, k_block, segment_ids, block_live):
    query_pos = q_block * T_DEV + jnp.arange(T_DEV, dtype=jnp.int32)
    key_pos = k_block * T_DEV + jnp.arange(T_DEV, dtype=jnp.int32)
    query_seg = lax.dynamic_slice_in_dim(segment_ids, q_block * T_DEV, T_DEV)
    key_seg = lax.dynamic_slice_in_dim(segment_ids, k_block * T_DEV, T_DEV)
    block_on = (k_block == q_block) | (k_block < q_block) & (block_live[q_block, k_block] == 1)
    allowed = (query_seg[:, None] == key_seg[None, :]) & (key_pos[None, :] <= query_pos[:, None]) & block_on
    return (allowed, block_on)

def block_scores(q_rows, k_rows):
    query_f32 = q_rows.astype(jnp.float32).reshape(T_DEV, HEADS, HD)
    key_f32 = k_rows.astype(jnp.float32).reshape(T_DEV, HEADS, HD)
    scores = jnp.einsum('qhd,khd->hqk', query_f32, key_f32, precision=lax.Precision.HIGHEST)
    return scores * (1.0 / math.sqrt(HD))

def attend_rows(q_block, queries, stretch_keys, stretch_values, segment_ids, block_live):
    q_rows = lax.dynamic_slice_in_dim(queries, q_block * T_DEV, T_DEV, 0)
    block_ids = jnp.arange(NBLK, dtype=jnp.int32)

    def max_step(row_best, k_block):
        allowed, block_on = block_allowed(q_block, k_block, segment_ids, block_live)

        def compute(current):
            k_rows = lax.dynamic_slice_in_dim(stretch_keys, k_block * T_DEV, T_DEV, 0)
            scores = block_scores(q_rows, k_rows)
            masked = jnp.where(allowed[None], scores, -jnp.inf)
            return jnp.maximum(current, lax.optimization_barrier(jnp.max(masked, axis=-1)))
        return (lax.cond(block_on, compute, lambda unchanged: unchanged, row_best), None)
    row_best, _ = lax.scan(max_step, jnp.full((HEADS, T_DEV), -jnp.inf, jnp.float32), block_ids)

    def sum_step(running, k_block):
        allowed, block_on = block_allowed(q_block, k_block, segment_ids, block_live)

        def compute(current):
            numerator, weight_sum = current
            k_rows = lax.dynamic_slice_in_dim(stretch_keys, k_block * T_DEV, T_DEV, 0)
            v_rows = lax.dynamic_slice_in_dim(stretch_values, k_block * T_DEV, T_DEV, 0)
            scores = block_scores(q_rows, k_rows)
            weights = jnp.where(allowed[None], jnp.exp(scores - row_best[..., None]), jnp.float32(0.0))
            weight_sum = weight_sum + lax.optimization_barrier(jnp.sum(weights, axis=-1))
            rounded = lax.optimization_barrier(weights.astype(jnp.bfloat16)).astype(jnp.float32)
            value_f32 = v_rows.astype(jnp.float32).reshape(T_DEV, HEADS, HD)
            numerator = numerator + jnp.einsum('hqk,khd->hqd', rounded, value_f32, precision=lax.Precision.HIGHEST)
            return (numerator, weight_sum)
        return (lax.cond(block_on, compute, lambda unchanged: unchanged, running), None)
    initial = (jnp.zeros((HEADS, T_DEV, HD), jnp.float32), jnp.zeros((HEADS, T_DEV), jnp.float32))
    (numerator, weight_sum), _ = lax.scan(sum_step, initial, block_ids)
    attended = numerator / weight_sum[..., None]
    return jnp.transpose(attended, (1, 0, 2)).reshape(T_DEV, HEADS * HD).astype(jnp.bfloat16)

def reference(queries, stretch_keys, stretch_values, segment_ids, block_live, out_weight, cache_keys, cache_values, page_table):
    blocks = lax.map(lambda q_block: attend_rows(q_block, queries, stretch_keys, stretch_values, segment_ids, block_live), jnp.arange(NBLK, dtype=jnp.int32))
    attn_out = blocks.reshape(TOKENS, HEADS * HD)
    group_width = HEADS * HD // N_HEAD

    def add_group(total_sum, group_idx):
        columns = lax.dynamic_slice_in_dim(attn_out, group_idx * group_width, group_width, 1)
        weight_rows = lax.dynamic_slice_in_dim(out_weight, group_idx * group_width, group_width, 0)
        partial_value = jnp.dot(columns, weight_rows, preferred_element_type=jnp.float32)
        partial_value = lax.optimization_barrier(partial_value.astype(jnp.bfloat16)).astype(jnp.float32)
        return (total_sum + partial_value, None)
    projected, _ = lax.scan(add_group, jnp.zeros((TOKENS, D), jnp.float32), jnp.arange(N_HEAD, dtype=jnp.int32))
    proj_out = projected.astype(jnp.bfloat16)

    def placed(cache):
        paged = cache.reshape(LAYERS_KV, NPAGES, PAGE, HEADS * HD)
        return jnp.zeros_like(paged).at[:, page_table].set(paged)
    return (attn_out, proj_out, placed(cache_keys), placed(cache_values))
```

```python
import functools
import math

import jax
import jax.numpy as jnp
from jax import lax
from jax.experimental import pallas as pl
from jax.experimental.pallas import tpu as pltpu
from jax.sharding import PartitionSpec as P

HD = 128
NZ = 4
SCORE_SCALE = 1.0 / math.sqrt(HD)
LOG2E = 1.4426950408889634
VMEM_LIMIT = 40 * 1024 * 1024


def copy_kernel(order_ref, src_ref, dst_ref):
    dst_ref[...] = src_ref[...].reshape(dst_ref.shape)


def gather_runs(cache, run_order, groups):
    layers, block_rows, feat = cache.shape
    run_rows = block_rows // groups
    return pl.pallas_call(
        copy_kernel,
        grid_spec=pltpu.PrefetchScalarGridSpec(
            num_scalar_prefetch=1,
            grid=(groups,),
            in_specs=[pl.BlockSpec((layers, run_rows, feat), lambda g, order: (0, order[g], 0))],
            out_specs=pl.BlockSpec((1, layers, run_rows, feat), lambda g, order: (g, 0, 0, 0)),
        ),
        out_shape=jax.ShapeDtypeStruct((groups, layers, run_rows, feat), cache.dtype),
        compiler_params=pltpu.CompilerParams(vmem_limit_bytes=VMEM_LIMIT),
        cost_estimate=pl.CostEstimate(flops=0, bytes_accessed=cache.size * 4, transcendentals=0),
        name="gather_runs",
    )(run_order, cache)


def place_kernel(order_ref, src_ref, dst_ref):
    dst_ref[...] = src_ref[...].reshape(dst_ref.shape)


def place_pages(moved, inverse, page_len):
    groups, layers, run_rows, feat = moved.shape
    per_group = run_rows // page_len
    page_count = groups * per_group
    return pl.pallas_call(
        place_kernel,
        grid_spec=pltpu.PrefetchScalarGridSpec(
            num_scalar_prefetch=1,
            grid=(page_count,),
            in_specs=[
                pl.BlockSpec(
                    (1, layers, page_len, feat),
                    lambda s, order: (order[s] // per_group, 0, order[s] % per_group, 0),
                )
            ],
            out_specs=pl.BlockSpec((layers, 1, page_len, feat), lambda s, order: (0, s, 0, 0)),
        ),
        out_shape=jax.ShapeDtypeStruct((layers, page_count, page_len, feat), moved.dtype),
        compiler_params=pltpu.CompilerParams(vmem_limit_bytes=VMEM_LIMIT),
        cost_estimate=pl.CostEstimate(flops=0, bytes_accessed=moved.size * 4, transcendentals=0),
        name="place_pages",
    )(inverse, moved)


def attend_kernel(count, first, last, *refs):
    flag_ref, block_ref, seg_col_ref, seg_ref, q_ref = refs[:5]
    kv = refs[5 : 5 + 2 * count]
    rest = refs[5 + 2 * count :]
    if first:
        outs = rest
    else:
        acc_in, m_in, l_in = rest[:3]
        outs = rest[3:]
    if last:
        o_ref, acc, m, l = outs
    else:
        acc, m, l = outs
    rows = q_ref.shape[0]
    if not first:
        acc[...] = acc_in[...]
        m[...] = m_in[...]
        l[...] = l_in[...]

    def step(i):
        k, v = kv[2 * i], kv[2 * i + 1]
        s = lax.dot_general(
            q_ref[...], k[...], (((1,), (1,)), ((), ())), preferred_element_type=jnp.float32
        )
        allowed = seg_col_ref[...] == seg_ref[block_ref[i]]
        initial = first and i == 0
        if initial:
            row = lax.broadcasted_iota(jnp.int32, s.shape, 0)
            col = lax.broadcasted_iota(jnp.int32, s.shape, 1)
            allowed = allowed & (col <= row)
        s = jnp.where(allowed, s, -jnp.inf)
        best = jnp.max(s, axis=1, keepdims=True)
        if not initial:
            old = m[0][:, :1]
            best = jnp.maximum(old, best)
        p = jnp.exp2((s - best) * (SCORE_SCALE * LOG2E))
        total = jnp.sum(p, axis=1, keepdims=True)
        pv = jnp.dot(p.astype(jnp.bfloat16), v[...], preferred_element_type=jnp.float32)
        if not initial:
            keep = jnp.exp2((old - best) * (SCORE_SCALE * LOG2E))
            total = l[0][:, :1] * keep + total
            pv = acc[0] * keep + pv
        acc[0] = pv
        m[0] = jnp.broadcast_to(best, (rows, HD))
        l[0] = jnp.broadcast_to(total, (rows, HD))

    for i in range(count):
        if first and i == 0:
            step(i)
        else:
            pl.when(flag_ref[i] == 1)(functools.partial(step, i))
    if last:
        o_ref[...] = (acc[0] / l[0]).astype(o_ref.dtype)


def attend(queries, pieces, sources, info, state, last):
    position, seg_blocks, live_row = info
    rows, feat = queries.shape
    heads = feat // HD
    first = state is None
    count = len(pieces)
    groups = seg_blocks.shape[0]
    blocks = jnp.stack([jnp.clip(b, 0, groups - 1) for b, _ in sources]).astype(jnp.int32)
    valid = jnp.stack([ok for _, ok in sources])
    reaches = seg_blocks[blocks, 0, rows - 1] == seg_blocks[position, 0, 0]
    flags = (valid & (blocks < position) & (live_row[blocks] == 1) & reaches).astype(jnp.int32)
    seg_col = seg_blocks[position, 0].reshape(rows, 1)
    head_spec = pl.BlockSpec((rows, HD), lambda h: (0, h))
    state_spec = pl.BlockSpec((1, rows, HD), lambda h: (h, 0, 0))
    smem = pl.BlockSpec(memory_space=pltpu.SMEM)
    in_specs = [
        smem,
        smem,
        pl.BlockSpec((rows, 1), lambda h: (0, 0)),
        pl.BlockSpec(seg_blocks.shape, lambda h: (0, 0, 0)),
        head_spec,
    ] + [head_spec] * (2 * count)
    args = [flags, blocks, seg_col, seg_blocks, queries]
    for k, v in pieces:
        args += [k, v]
    if not first:
        in_specs += [state_spec] * 3
        args += list(state)
    state_shape = jax.ShapeDtypeStruct((heads, rows, HD), jnp.float32)
    scratch = []
    if last:
        out_shape = jax.ShapeDtypeStruct((rows, feat), jnp.bfloat16)
        out_specs = head_spec
        scratch = [pltpu.VMEM((1, rows, HD), jnp.float32)] * 3
    else:
        out_shape = (state_shape,) * 3
        out_specs = (state_spec,) * 3
    return pl.pallas_call(
        functools.partial(attend_kernel, count, first, last),
        grid=(heads,),
        in_specs=in_specs,
        out_specs=out_specs,
        out_shape=out_shape,
        scratch_shapes=scratch,
        compiler_params=pltpu.CompilerParams(vmem_limit_bytes=VMEM_LIMIT),
        cost_estimate=pl.CostEstimate(
            flops=count * heads * rows * rows * HD * 4,
            bytes_accessed=count * rows * feat * 4 + 6 * heads * rows * HD * 4,
            transcendentals=count * heads * rows * rows,
        ),
        name="attend",
    )(*args)


def local(
    queries,
    stretch_keys,
    stretch_values,
    segment_ids,
    block_live,
    out_weight,
    cache_keys,
    cache_values,
    page_table,
):
    groups = lax.axis_size("seq")
    position = lax.axis_index("seq")
    ny = groups // NZ
    rows = queries.shape[0]
    z, y = position // ny, position % ny
    live_row = lax.dynamic_index_in_dim(block_live, position, 0, keepdims=False)
    info = (position, segment_ids.reshape(groups, 1, rows), live_row)

    def move(pair, links):
        return tuple(lax.ppermute(part, "seq", links) for part in pair)

    def up(span):
        return [(a * ny + c, (a + 1) * ny + c) for a in range(span - 1, NZ - 1) for c in range(ny)]

    def across(shift, span):
        return [
            (a * ny + c, a * ny + (c + shift) % ny)
            for a in range(span, NZ)
            for c in range(ny)
            if span > 0 or c + shift < ny
        ]

    page_count = page_table.shape[0] // groups
    page_len = cache_keys.shape[1] // page_count
    per_group = page_count // groups
    slot_table = page_table.reshape(groups, page_count)
    owner = slot_table[:, ::per_group] // page_count
    own_runs = lax.dynamic_index_in_dim(owner, position, 0, keepdims=False)
    ids = jnp.arange(groups, dtype=jnp.int32)
    run_order = jnp.sum(
        jnp.where(own_runs[None, :] == ids[:, None], ids[None, :], 0), axis=1
    ).astype(jnp.int32)
    here = slot_table // page_count == position
    arrival = ids[:, None] * per_group + jnp.arange(page_count, dtype=jnp.int32)[None, :] % per_group
    slots = jnp.arange(page_count, dtype=jnp.int32)
    match = here[None] & (slot_table[None] % page_count == slots[:, None, None])
    inverse = jnp.sum(jnp.where(match, arrival[None], 0), axis=(1, 2)).astype(jnp.int32)

    own = (stretch_keys, stretch_values)
    level = {0: own}
    for span in range(1, NZ):
        level[span] = move(level[span - 1], up(span))
    side = {
        (span, shift): move(level[span], across(shift, span))
        for span in range(NZ)
        for shift in range(1, ny)
    }

    def exchange(cache, after):
        ordered = gather_runs(cache, run_order, groups)
        if after is not None:
            ordered, _ = lax.optimization_barrier((ordered, after))
        return lax.all_to_all(ordered, "seq", split_axis=0, concat_axis=0, tiled=True)

    moved_keys = exchange(cache_keys, level[1][0])
    moved_values = exchange(cache_values, level[3][1])

    def source(span, shift=0):
        column = (y - shift) % ny
        return ((z - span) * ny + column, z >= span)

    state = attend(queries, [own], [source(0)], info, None, False)
    for span in range(NZ):
        pieces = [side[span, shift] for shift in range(1, ny)]
        sources = [source(span, shift) for shift in range(1, ny)]
        if span + 1 < NZ:
            pieces.append(level[span + 1])
            sources.append(source(span + 1))
        state = attend(queries, pieces, sources, info, state, span + 1 == NZ)
    attended = state
    projected = lax.psum_scatter(
        jnp.dot(attended, out_weight, preferred_element_type=jnp.float32).astype(jnp.bfloat16),
        "head",
        scatter_dimension=0,
        tiled=True,
    )
    decode_keys = place_pages(moved_keys, inverse, page_len)
    decode_values = place_pages(moved_values, inverse, page_len)
    return (attended, projected, decode_keys, decode_values)


def solution(mesh):
    placed = (
        P("seq", "head"),
        P("seq", "head"),
        P("seq", "head"),
        P(),
        P(),
        P("head", None),
        P(None, "seq", "head"),
        P(None, "seq", "head"),
        P(),
    )
    return jax.shard_map(
        local,
        mesh=mesh,
        in_specs=placed,
        out_specs=(
            P("seq", "head"),
            P(("seq", "head"), None),
            P(None, "seq", None, "head"),
            P(None, "seq", None, "head"),
        ),
        check_vma=False,
    )
```

```python
import functools
import math

import jax
import jax.numpy as jnp
import numpy as np
from jax import lax
from jax.experimental import pallas as pl
from jax.experimental.pallas import tpu as pltpu
from jax.sharding import PartitionSpec as P

HD = 128
NZ = 4
SCORE_SCALE = 1.0 / math.sqrt(HD)
LOG2E = 1.4426950408889634
VMEM_LIMIT = 60 * 1024 * 1024


def pack_kernel(count, run_rows, flag_ref, run_ref, keys_ref, values_ref, *refs):
    outs, (buffer, in_sem, out_sem) = refs[:count], refs[count:]
    layers = keys_ref.shape[0]

    def load(j):
        rows = pl.ds(pl.multiple_of(run_ref[j] * run_rows, run_rows), run_rows)
        for part, cache in enumerate((keys_ref, values_ref)):
            pltpu.make_async_copy(
                cache.at[:, rows, :], buffer.at[j, pl.ds(part * layers, layers)], in_sem.at[j]
            ).start()

    def store(j):
        pltpu.make_async_copy(outs[j], buffer.at[j], in_sem.at[j]).wait()
        pltpu.make_async_copy(buffer.at[j], outs[j], out_sem.at[j]).start()

    def finish(j):
        pltpu.make_async_copy(buffer.at[j], outs[j], out_sem.at[j]).wait()

    for stage in (load, store, finish):
        for j in range(count):
            pl.when(flag_ref[j] == 1)(functools.partial(stage, j))


def pack_runs(cache_keys, cache_values, flags, runs, groups):
    count = flags.shape[0]
    layers, block_rows, feat = cache_keys.shape
    run_rows = block_rows // groups
    slab = (2 * layers, run_rows, feat)
    smem, hbm = pl.BlockSpec(memory_space=pltpu.SMEM), pl.BlockSpec(memory_space=pl.ANY)
    return pl.pallas_call(
        functools.partial(pack_kernel, count, run_rows),
        in_specs=[smem, smem, hbm, hbm],
        out_specs=[hbm] * count,
        out_shape=[jax.ShapeDtypeStruct(slab, cache_keys.dtype)] * count,
        scratch_shapes=[
            pltpu.VMEM((count,) + slab, cache_keys.dtype),
            pltpu.SemaphoreType.DMA((count,)),
            pltpu.SemaphoreType.DMA((count,)),
        ],
        compiler_params=pltpu.CompilerParams(vmem_limit_bytes=VMEM_LIMIT),
        cost_estimate=pl.CostEstimate(
            flops=0, bytes_accessed=cache_keys.size * 8, transcendentals=0
        ),
        name="pack_runs",
    )(flags, runs, cache_keys, cache_values)


def place_kernel(count, page_len, flag_ref, slot_ref, run_ref, *refs):
    slabs = refs[:count]
    keys_ref, values_ref, keys_out, values_out, buffer, in_sem, out_sem = refs[count:]
    layers, _, feat = keys_ref.shape
    run_rows = buffer.shape[2]

    def load(j):
        if j < count:
            pltpu.make_async_copy(slabs[j], buffer.at[j], in_sem.at[j]).start()
            return
        rows = pl.ds(pl.multiple_of(run_ref[0] * run_rows, run_rows), run_rows)
        for part, cache in enumerate((keys_ref, values_ref)):
            pltpu.make_async_copy(
                cache.at[:, rows, :], buffer.at[j, pl.ds(part * layers, layers)], in_sem.at[j]
            ).start()

    def store(j):
        pltpu.make_async_copy(slabs[0], buffer.at[j], in_sem.at[j]).wait()
        for page in range(run_rows // page_len):
            rows = pl.ds(page * page_len, page_len)
            for part, out in enumerate((keys_out, values_out)):
                pltpu.make_async_copy(
                    buffer.at[j, pl.ds(part * layers, layers), rows, :],
                    out.at[:, slot_ref[j, page]],
                    out_sem.at[part],
                ).start()

    for stage in (load, store):
        for j in range(count + 1):
            pl.when(flag_ref[j] == 1)(functools.partial(stage, j))
    for part, out in enumerate((keys_out, values_out)):
        pltpu.make_async_copy(out, out, out_sem.at[part]).wait()


def place_pages(slabs, cache_keys, cache_values, flags, slots, own_run, page_len):
    count = len(slabs)
    layers, block_rows, feat = cache_keys.shape
    out_shape = jax.ShapeDtypeStruct(
        (layers, block_rows // page_len, page_len, feat), cache_keys.dtype
    )
    smem, hbm = pl.BlockSpec(memory_space=pltpu.SMEM), pl.BlockSpec(memory_space=pl.ANY)
    return pl.pallas_call(
        functools.partial(place_kernel, count, page_len),
        in_specs=[smem] * 3 + [hbm] * (count + 2),
        out_specs=[hbm] * 2,
        out_shape=[out_shape] * 2,
        scratch_shapes=[
            pltpu.VMEM((count + 1,) + slabs[0].shape, cache_keys.dtype),
            pltpu.SemaphoreType.DMA((count + 1,)),
            pltpu.SemaphoreType.DMA((2,)),
        ],
        compiler_params=pltpu.CompilerParams(vmem_limit_bytes=VMEM_LIMIT),
        cost_estimate=pl.CostEstimate(
            flops=0, bytes_accessed=cache_keys.size * 8, transcendentals=0
        ),
        name="place_pages",
    )(flags, slots, own_run, *slabs, cache_keys, cache_values)


def page_sends(ny):
    sends = [(0, [(1, 0), (2, 1), (3, 2)], 0), (0, [(2, 0), (3, 1)], 0)]
    sends += [(2, [(0, 1), (1, 2), (3, 0)], 0), (2, [(0, 2)], 0)]
    sends += [(3, [(2, 3)], 0), (4, [(1, 3)], 0), (4, [(0, 3)], 0)]
    for dy in range(1, ny):
        sends += [
            (0, [(0, 0), (1, 1), (2, 2), (3, 3)], dy),
            (2, [(1, 0), (2, 1), (3, 2)], dy),
            (3, [(0, 1), (1, 2), (3, 0)], dy),
            (3, [(0, 2), (2, 0), (3, 1)], dy),
            (4, [(2, 3)], dy),
            (5, [(1, 3)], dy),
            (5, [(0, 3)], dy),
        ]
    return sorted(sends, key=lambda send: send[0])


def attend_kernel(count, first, last, *refs):
    flag_ref, block_ref, seg_col_ref, seg_ref, q_ref = refs[:5]
    kv = refs[5 : 5 + 2 * count]
    rest = refs[5 + 2 * count :]
    if first:
        outs = rest
    else:
        acc_in, m_in, l_in = rest[:3]
        outs = rest[3:]
    if last:
        o_ref, acc, m, l = outs
    else:
        acc, m, l = outs
    rows = q_ref.shape[0]
    if not first:
        acc[...] = acc_in[...]
        m[...] = m_in[...]
        l[...] = l_in[...]

    def step(i):
        k, v = kv[2 * i], kv[2 * i + 1]
        s = lax.dot_general(
            q_ref[...], k[...], (((1,), (1,)), ((), ())), preferred_element_type=jnp.float32
        )
        allowed = seg_col_ref[...] == seg_ref[block_ref[i]]
        initial = first and i == 0
        if initial:
            row = lax.broadcasted_iota(jnp.int32, s.shape, 0)
            col = lax.broadcasted_iota(jnp.int32, s.shape, 1)
            allowed = allowed & (col <= row)
        s = jnp.where(allowed, s, -jnp.inf)
        best = jnp.max(s, axis=1, keepdims=True)
        if not initial:
            old = m[0][:, :1]
            best = jnp.maximum(old, best)
        p = jnp.exp2((s - best) * (SCORE_SCALE * LOG2E))
        total = jnp.sum(p, axis=1, keepdims=True)
        pv = jnp.dot(p.astype(jnp.bfloat16), v[...], preferred_element_type=jnp.float32)
        if not initial:
            keep = jnp.exp2((old - best) * (SCORE_SCALE * LOG2E))
            total = l[0][:, :1] * keep + total
            pv = acc[0] * keep + pv
        acc[0] = pv
        m[0] = jnp.broadcast_to(best, (rows, HD))
        l[0] = jnp.broadcast_to(total, (rows, HD))

    for i in range(count):
        if first and i == 0:
            step(i)
        else:
            pl.when(flag_ref[i] == 1)(functools.partial(step, i))
    if last:
        o_ref[...] = (acc[0] / l[0]).astype(o_ref.dtype)


def attend(queries, pieces, sources, info, state, last):
    position, seg_blocks, live_row = info
    rows, feat = queries.shape
    heads = feat // HD
    first = state is None
    count = len(pieces)
    groups = seg_blocks.shape[0]
    blocks = jnp.stack([jnp.clip(b, 0, groups - 1) for b, _ in sources]).astype(jnp.int32)
    valid = jnp.stack([ok for _, ok in sources])
    reaches = seg_blocks[blocks, 0, rows - 1] == seg_blocks[position, 0, 0]
    flags = (valid & (blocks < position) & (live_row[blocks] == 1) & reaches).astype(jnp.int32)
    seg_col = seg_blocks[position, 0].reshape(rows, 1)
    head_spec = pl.BlockSpec((rows, HD), lambda h: (0, h))
    value_spec = pl.BlockSpec((rows, HD), lambda h: (1, h))
    state_spec = pl.BlockSpec((1, rows, HD), lambda h: (h, 0, 0))
    smem = pl.BlockSpec(memory_space=pltpu.SMEM)
    in_specs = [
        smem,
        smem,
        pl.BlockSpec((rows, 1), lambda h: (0, 0)),
        pl.BlockSpec(seg_blocks.shape, lambda h: (0, 0, 0)),
        head_spec,
    ] + [head_spec, value_spec] * count
    args = [flags, blocks, seg_col, seg_blocks, queries]
    for piece in pieces:
        args += [piece, piece]
    if not first:
        in_specs += [state_spec] * 3
        args += list(state)
    state_shape = jax.ShapeDtypeStruct((heads, rows, HD), jnp.float32)
    scratch = []
    if last:
        out_shape = jax.ShapeDtypeStruct((rows, feat), jnp.bfloat16)
        out_specs = head_spec
        scratch = [pltpu.VMEM((1, rows, HD), jnp.float32)] * 3
    else:
        out_shape = (state_shape,) * 3
        out_specs = (state_spec,) * 3
    return pl.pallas_call(
        functools.partial(attend_kernel, count, first, last),
        grid=(heads,),
        in_specs=in_specs,
        out_specs=out_specs,
        out_shape=out_shape,
        scratch_shapes=scratch,
        compiler_params=pltpu.CompilerParams(vmem_limit_bytes=VMEM_LIMIT),
        cost_estimate=pl.CostEstimate(
            flops=count * heads * rows * rows * HD * 4,
            bytes_accessed=count * rows * feat * 4 + 6 * heads * rows * HD * 4,
            transcendentals=count * heads * rows * rows,
        ),
        name="attend",
    )(*args)


def reduce_rows(partial):
    size = lax.axis_size("head")
    index = lax.axis_index("head")
    rows, width = partial.shape
    part = partial.reshape(1, size, rows // size, width)
    bit = 1
    while bit < size:
        part = part.reshape(size // (2 * bit), 2, rows // size, width)
        mine = (index // bit) % 2
        away = lax.dynamic_index_in_dim(part, 1 - mine, 1, keepdims=False)
        keep = lax.dynamic_index_in_dim(part, mine, 1, keepdims=False)
        links = [(a, a ^ bit) for a in range(size)]
        taken = lax.ppermute(away.astype(jnp.bfloat16), "head", links)
        part = keep.astype(jnp.float32) + taken.astype(jnp.float32)
        bit *= 2
    return part.reshape(rows // size, width).astype(jnp.bfloat16)


def local(
    queries,
    stretch_keys,
    stretch_values,
    segment_ids,
    block_live,
    out_weight,
    cache_keys,
    cache_values,
    page_table,
):
    groups = lax.axis_size("seq")
    position = lax.axis_index("seq")
    ny = groups // NZ
    rows = queries.shape[0]
    z, y = position // ny, position % ny
    live_row = lax.dynamic_index_in_dim(block_live, position, 0, keepdims=False)
    info = (position, segment_ids.reshape(groups, 1, rows), live_row)

    def up(span):
        return [(a * ny + c, (a + 1) * ny + c) for a in range(span - 1, NZ - 1) for c in range(ny)]

    def across(shift, span):
        return [
            (a * ny + c, a * ny + (c + shift) % ny)
            for a in range(span, NZ)
            for c in range(ny)
            if span > 0 or c + shift < ny
        ]

    page_count = page_table.shape[0] // groups
    page_len = cache_keys.shape[1] // page_count
    per_group = page_count // groups
    slot_table = page_table.reshape(groups, page_count)
    owner = slot_table[:, ::per_group] // page_count
    ids = jnp.arange(groups, dtype=jnp.int32)
    sends = page_sends(ny)
    target_z = np.full((len(sends) + 1, NZ), -1, np.int32)
    origin_z = np.full((len(sends) + 1, NZ), -1, np.int32)
    shifts = np.array([dy for _, _, dy in sends] + [0], np.int32)
    for j, (_, moves, _) in enumerate(sends):
        for a, b in moves:
            target_z[j, a], origin_z[j, b] = b, a
    target_z[-1] = origin_z[-1] = np.arange(NZ)
    to_z, from_z = jnp.asarray(target_z)[:, z], jnp.asarray(origin_z)[:, z]
    target = jnp.maximum(to_z, 0) * ny + (y + shifts) % ny
    origin = jnp.maximum(from_z, 0) * ny + (y - shifts) % ny
    own_runs = lax.dynamic_index_in_dim(owner, position, 0, keepdims=False)
    runs = jnp.sum(
        jnp.where(own_runs[None, :] == target[:, None], ids[None, :], 0), axis=1
    ).astype(jnp.int32)
    comes = owner[origin] == position
    origin_slots = (slot_table[origin] % page_count).reshape(-1, groups, per_group)
    slots = jnp.sum(jnp.where(comes[:, :, None], origin_slots, 0), axis=1).astype(jnp.int32)
    send_flags = (to_z >= 0).astype(jnp.int32)
    take_flags = (from_z >= 0).astype(jnp.int32)

    packed = pack_runs(cache_keys, cache_values, send_flags[:-1], runs[:-1], groups)
    own = jnp.concatenate([stretch_keys, stretch_values], axis=0)
    blocks = {("up", 0): own}

    slabs, arrived = {}, []
    for phase in range(6):
        chosen = [j for j, send in enumerate(sends) if send[0] == phase]
        ready = [packed[j] for j in chosen]
        if phase < NZ:
            block = blocks["up", phase]
            block, ready, _ = lax.optimization_barrier((block, ready, arrived))
            if phase + 1 < NZ:
                blocks["up", phase + 1] = lax.ppermute(block, "seq", up(phase + 1))
            for shift in range(1, ny):
                blocks[phase, shift] = lax.ppermute(block, "seq", across(shift, phase))
        else:
            if phase == NZ:
                for shift in range(1, ny):
                    block = blocks[NZ - 1, shift]
                    blocks[NZ - 1, shift], _ = lax.optimization_barrier((block, arrived))
            ready, _ = lax.optimization_barrier((ready, arrived))
        for j, slab in zip(chosen, ready):
            _, moves, dy = sends[j]
            links = [(a * ny + c, b * ny + (c + dy) % ny) for a, b in moves for c in range(ny)]
            slabs[j] = lax.ppermute(slab, "seq", links)
        if phase == 0:
            held = [slabs[j] for j in chosen]
        else:
            arrived = [slabs[j] for j in chosen] if phase > 1 else held
    slabs = [slabs[j] for j in range(len(sends))]

    def source(span, shift=0):
        column = (y - shift) % ny
        return ((z - span) * ny + column, z >= span)

    state = attend(queries, [own], [source(0)], info, None, False)
    for span in range(NZ):
        pieces = [blocks[span, shift] for shift in range(1, ny)]
        sources = [source(span, shift) for shift in range(1, ny)]
        if span + 1 < NZ:
            pieces.append(blocks["up", span + 1])
            sources.append(source(span + 1))
        state = attend(queries, pieces, sources, info, state, span + 1 == NZ)
    attended = state
    partial = jnp.dot(attended, out_weight, preferred_element_type=jnp.float32)
    projected = reduce_rows(partial.astype(jnp.bfloat16))
    decode_keys, decode_values = place_pages(
        slabs, cache_keys, cache_values, take_flags, slots, runs[-1:], page_len
    )
    return (attended, projected, decode_keys, decode_values)


def solution(mesh):
    placed = (
        P("seq", "head"),
        P("seq", "head"),
        P("seq", "head"),
        P(),
        P(),
        P("head", None),
        P(None, "seq", "head"),
        P(None, "seq", "head"),
        P(),
    )
    return jax.shard_map(
        local,
        mesh=mesh,
        in_specs=placed,
        out_specs=(
            P("seq", "head"),
            P(("seq", "head"), None),
            P(None, "seq", None, "head"),
            P(None, "seq", None, "head"),
        ),
        check_vma=False,
    )
```

```python
import functools
import math

import jax
import jax.numpy as jnp
from jax import lax
from jax.experimental import pallas as pl
from jax.experimental.pallas import tpu as pltpu
from jax.sharding import PartitionSpec as P

HD = 128
NZ = 4
SCORE_SCALE = 1.0 / math.sqrt(HD)
LOG2E = 1.4426950408889634
VMEM_LIMIT = 40 * 1024 * 1024


def copy_kernel(order_ref, src_ref, dst_ref):
    dst_ref[...] = src_ref[...].reshape(dst_ref.shape)


def gather_runs(cache, run_order, groups):
    layers, block_rows, feat = cache.shape
    run_rows = block_rows // groups
    return pl.pallas_call(
        copy_kernel,
        grid_spec=pltpu.PrefetchScalarGridSpec(
            num_scalar_prefetch=1,
            grid=(groups,),
            in_specs=[pl.BlockSpec((layers, run_rows, feat), lambda g, order: (0, order[g], 0))],
            out_specs=pl.BlockSpec((1, layers, run_rows, feat), lambda g, order: (g, 0, 0, 0)),
        ),
        out_shape=jax.ShapeDtypeStruct((groups, layers, run_rows, feat), cache.dtype),
        compiler_params=pltpu.CompilerParams(vmem_limit_bytes=VMEM_LIMIT),
        cost_estimate=pl.CostEstimate(flops=0, bytes_accessed=cache.size * 4, transcendentals=0),
        name="gather_runs",
    )(run_order, cache)


def place_kernel(page_len, slot_ref, moved_ref, out_ref, buffer, in_sem, out_sem):
    groups, _, run_rows, _ = moved_ref.shape

    def load(g):
        return pltpu.make_async_copy(moved_ref.at[g], buffer.at[g], in_sem.at[g])

    for g in range(groups):
        load(g).start()
    for g in range(groups):
        load(g).wait()
        for page in range(run_rows // page_len):
            pltpu.make_async_copy(
                buffer.at[g, :, pl.ds(page * page_len, page_len), :],
                out_ref.at[:, slot_ref[g, page]],
                out_sem,
            ).start()
    pltpu.make_async_copy(out_ref, out_ref, out_sem).wait()


def place_pages(moved, slots, page_len):
    groups, layers, run_rows, feat = moved.shape
    page_count = groups * run_rows // page_len
    return pl.pallas_call(
        functools.partial(place_kernel, page_len),
        in_specs=[pl.BlockSpec(memory_space=pltpu.SMEM), pl.BlockSpec(memory_space=pl.ANY)],
        out_specs=pl.BlockSpec(memory_space=pl.ANY),
        out_shape=jax.ShapeDtypeStruct((layers, page_count, page_len, feat), moved.dtype),
        scratch_shapes=[
            pltpu.VMEM(moved.shape, moved.dtype),
            pltpu.SemaphoreType.DMA((groups,)),
            pltpu.SemaphoreType.DMA,
        ],
        compiler_params=pltpu.CompilerParams(vmem_limit_bytes=VMEM_LIMIT),
        cost_estimate=pl.CostEstimate(flops=0, bytes_accessed=moved.size * 4, transcendentals=0),
        name="place_pages",
    )(slots, moved)


def attend_kernel(count, first, last, *refs):
    flag_ref, block_ref, seg_col_ref, seg_ref, q_ref = refs[:5]
    kv = refs[5 : 5 + 2 * count]
    rest = refs[5 + 2 * count :]
    if first:
        outs = rest
    else:
        acc_in, m_in, l_in = rest[:3]
        outs = rest[3:]
    if last:
        o_ref, acc, m, l = outs
    else:
        acc, m, l = outs
    rows = q_ref.shape[0]
    if not first:
        acc[...] = acc_in[...]
        m[...] = m_in[...]
        l[...] = l_in[...]

    def step(i):
        k, v = kv[2 * i], kv[2 * i + 1]
        s = lax.dot_general(
            q_ref[...], k[...], (((1,), (1,)), ((), ())), preferred_element_type=jnp.float32
        )
        allowed = seg_col_ref[...] == seg_ref[block_ref[i]]
        initial = first and i == 0
        if initial:
            row = lax.broadcasted_iota(jnp.int32, s.shape, 0)
            col = lax.broadcasted_iota(jnp.int32, s.shape, 1)
            allowed = allowed & (col <= row)
        s = jnp.where(allowed, s, -jnp.inf)
        best = jnp.max(s, axis=1, keepdims=True)
        if not initial:
            old = m[0][:, :1]
            best = jnp.maximum(old, best)
        p = jnp.exp2((s - best) * (SCORE_SCALE * LOG2E))
        total = jnp.sum(p, axis=1, keepdims=True)
        pv = jnp.dot(p.astype(jnp.bfloat16), v[...], preferred_element_type=jnp.float32)
        if not initial:
            keep = jnp.exp2((old - best) * (SCORE_SCALE * LOG2E))
            total = l[0][:, :1] * keep + total
            pv = acc[0] * keep + pv
        acc[0] = pv
        m[0] = jnp.broadcast_to(best, (rows, HD))
        l[0] = jnp.broadcast_to(total, (rows, HD))

    for i in range(count):
        if first and i == 0:
            step(i)
        else:
            pl.when(flag_ref[i] == 1)(functools.partial(step, i))
    if last:
        o_ref[...] = (acc[0] / l[0]).astype(o_ref.dtype)


def attend(queries, pieces, sources, info, state, last):
    position, seg_blocks, live_row = info
    rows, feat = queries.shape
    heads = feat // HD
    first = state is None
    count = len(pieces)
    groups = seg_blocks.shape[0]
    blocks = jnp.stack([jnp.clip(b, 0, groups - 1) for b, _ in sources]).astype(jnp.int32)
    valid = jnp.stack([ok for _, ok in sources])
    reaches = seg_blocks[blocks, 0, rows - 1] == seg_blocks[position, 0, 0]
    flags = (valid & (blocks < position) & (live_row[blocks] == 1) & reaches).astype(jnp.int32)
    seg_col = seg_blocks[position, 0].reshape(rows, 1)
    head_spec = pl.BlockSpec((rows, HD), lambda h: (0, h))
    state_spec = pl.BlockSpec((1, rows, HD), lambda h: (h, 0, 0))
    smem = pl.BlockSpec(memory_space=pltpu.SMEM)
    in_specs = [
        smem,
        smem,
        pl.BlockSpec((rows, 1), lambda h: (0, 0)),
        pl.BlockSpec(seg_blocks.shape, lambda h: (0, 0, 0)),
        head_spec,
    ] + [head_spec] * (2 * count)
    args = [flags, blocks, seg_col, seg_blocks, queries]
    for k, v in pieces:
        args += [k, v]
    if not first:
        in_specs += [state_spec] * 3
        args += list(state)
    state_shape = jax.ShapeDtypeStruct((heads, rows, HD), jnp.float32)
    scratch = []
    if last:
        out_shape = jax.ShapeDtypeStruct((rows, feat), jnp.bfloat16)
        out_specs = head_spec
        scratch = [pltpu.VMEM((1, rows, HD), jnp.float32)] * 3
    else:
        out_shape = (state_shape,) * 3
        out_specs = (state_spec,) * 3
    return pl.pallas_call(
        functools.partial(attend_kernel, count, first, last),
        grid=(heads,),
        in_specs=in_specs,
        out_specs=out_specs,
        out_shape=out_shape,
        scratch_shapes=scratch,
        compiler_params=pltpu.CompilerParams(vmem_limit_bytes=VMEM_LIMIT),
        cost_estimate=pl.CostEstimate(
            flops=count * heads * rows * rows * HD * 4,
            bytes_accessed=count * rows * feat * 4 + 6 * heads * rows * HD * 4,
            transcendentals=count * heads * rows * rows,
        ),
        name="attend",
    )(*args)


def reduce_rows(partial):
    size = lax.axis_size("head")
    index = lax.axis_index("head")
    rows, width = partial.shape
    part = partial.reshape(1, size, rows // size, width)
    bit = 1
    while bit < size:
        part = part.reshape(size // (2 * bit), 2, rows // size, width)
        mine = (index // bit) % 2
        away = lax.dynamic_index_in_dim(part, 1 - mine, 1, keepdims=False)
        keep = lax.dynamic_index_in_dim(part, mine, 1, keepdims=False)
        links = [(a, a ^ bit) for a in range(size)]
        taken = lax.ppermute(away.astype(jnp.bfloat16), "head", links)
        part = keep.astype(jnp.float32) + taken.astype(jnp.float32)
        bit *= 2
    return part.reshape(rows // size, width).astype(jnp.bfloat16)


def local(
    queries,
    stretch_keys,
    stretch_values,
    segment_ids,
    block_live,
    out_weight,
    cache_keys,
    cache_values,
    page_table,
):
    groups = lax.axis_size("seq")
    position = lax.axis_index("seq")
    ny = groups // NZ
    rows = queries.shape[0]
    z, y = position // ny, position % ny
    live_row = lax.dynamic_index_in_dim(block_live, position, 0, keepdims=False)
    info = (position, segment_ids.reshape(groups, 1, rows), live_row)

    def move(pair, links):
        return tuple(lax.ppermute(part, "seq", links) for part in pair)

    def up(span):
        return [(a * ny + c, (a + 1) * ny + c) for a in range(span - 1, NZ - 1) for c in range(ny)]

    def across(shift, span):
        return [
            (a * ny + c, a * ny + (c + shift) % ny)
            for a in range(span, NZ)
            for c in range(ny)
            if span > 0 or c + shift < ny
        ]

    page_count = page_table.shape[0] // groups
    page_len = cache_keys.shape[1] // page_count
    per_group = page_count // groups
    slot_table = page_table.reshape(groups, page_count)
    owner = slot_table[:, ::per_group] // page_count
    own_runs = lax.dynamic_index_in_dim(owner, position, 0, keepdims=False)
    ids = jnp.arange(groups, dtype=jnp.int32)
    run_order = jnp.sum(
        jnp.where(own_runs[None, :] == ids[:, None], ids[None, :], 0), axis=1
    ).astype(jnp.int32)
    comes = owner == position
    local_slots = (slot_table % page_count).reshape(groups, groups, per_group)
    slots = jnp.sum(jnp.where(comes[:, :, None], local_slots, 0), axis=1).astype(jnp.int32)

    own = (stretch_keys, stretch_values)

    def exchange(cache, after):
        ordered = gather_runs(cache, run_order, groups)
        if after is not None:
            ordered, _ = lax.optimization_barrier((ordered, after))
        return lax.all_to_all(ordered, "seq", split_axis=0, concat_axis=0, tiled=True)

    moved_keys = exchange(cache_keys, None)
    moved_values = exchange(cache_values, moved_keys)
    level = {0: own}
    for span in range(1, NZ):
        level[span] = move(level[span - 1], up(span))
    late, _ = lax.optimization_barrier((level[NZ - 1], moved_keys))
    side = {
        (span, shift): move(level[span] if span < NZ - 1 else late, across(shift, span))
        for span in range(NZ)
        for shift in range(1, ny)
    }

    def source(span, shift=0):
        column = (y - shift) % ny
        return ((z - span) * ny + column, z >= span)

    state = attend(queries, [own], [source(0)], info, None, False)
    for span in range(NZ):
        pieces = [side[span, shift] for shift in range(1, ny)]
        sources = [source(span, shift) for shift in range(1, ny)]
        if span + 1 < NZ:
            pieces.append(level[span + 1])
            sources.append(source(span + 1))
        state = attend(queries, pieces, sources, info, state, span + 1 == NZ)
    attended = state
    partial = jnp.dot(attended, out_weight, preferred_element_type=jnp.float32)
    projected = reduce_rows(partial.astype(jnp.bfloat16))
    decode_keys = place_pages(moved_keys, slots, page_len)
    decode_values = place_pages(moved_values, slots, page_len)
    return (attended, projected, decode_keys, decode_values)


def solution(mesh):
    placed = (
        P("seq", "head"),
        P("seq", "head"),
        P("seq", "head"),
        P(),
        P(),
        P("head", None),
        P(None, "seq", "head"),
        P(None, "seq", "head"),
        P(),
    )
    return jax.shard_map(
        local,
        mesh=mesh,
        in_specs=placed,
        out_specs=(
            P("seq", "head"),
            P(("seq", "head"), None),
            P(None, "seq", None, "head"),
            P(None, "seq", None, "head"),
        ),
        check_vma=False,
    )
```
